32 devices in a mesh: dcn: 4 (over y, x), ctx: 4 (over z), head: 2 (over core).
Axes of the slice: x: 2, y: 2, z: 4, core: 2. Of those that a mesh axis runs over, the one named last changes fastest.
Arguments:
- queries: bfloat16 [4096, 64, 128], P(('dcn', 'ctx'), 'head'), may hold values from -26 to 26
- keys: bfloat16 [4096, 8, 128], P(('dcn', 'ctx'), 'head'), may hold values from -6 to 6
- values: bfloat16 [4096, 8, 128], P(('dcn', 'ctx'), 'head'), may hold values from -6 to 6
- seg_ids: int32 [4096], P(('dcn', 'ctx')), may hold values from 0 to 15, never falling along the last dimension, each value on 1 to 768 neighbouring positions
Outputs:
- attended: bfloat16 [4096, 64, 128], P(('dcn', 'ctx'), 'head')
The draws below stay inside these ranges and needn't reach their ends.
Inputs may be any that keep to these rules, and one draw needn't show every extreme that they name: `seg_ids`: ids never fall along the sequence; every document has 1 to 768 tokens and one has exactly 768.
All inputs are finite; a program needn't handle non-finite values.
Results may differ from the reference program's by a relative error of at most 0.0025.
Values may be sent and summed in bfloat16 or wider, within the bound.
A program may use at most 64 MiB of HBM per device.

```python
import math
import jax
import jax.numpy as jnp
import numpy as np
from jax import lax

HD = 128
HEADS = 64
KV_HEADS = 8
STEPS = 3
TOK_DEV = 256
TOKENS = 4096
DOC_MAX = 768
NDOCS = 16


def paired_fields(key):
    base = jax.random.fold_in(key, 11)
    key_field = jnp.clip(jax.random.normal(jax.random.fold_in(base, 1), (TOKENS, KV_HEADS, HD), jnp.float32), -4.0, 4.0) * 1.5
    query_field = jnp.clip(jax.random.normal(jax.random.fold_in(base, 2), (TOKENS, HEADS, HD), jnp.float32), -4.0, 4.0) * 2.0
    return (query_field.astype(jnp.bfloat16), key_field.astype(jnp.bfloat16))


def draw_queries(key, part):
    return paired_fields(key)[0]


def draw_keys(key, part):
    return paired_fields(key)[1]


def level_of(rng, dims, pieces, smallest, top_value):
    loudness, own = 1.0, jax.random.fold_in(rng, 6)
    for position, blocks in pieces:
        steps = jnp.exp(jax.random.uniform(jax.random.fold_in(own, position), (blocks,), jnp.float32, smallest / len(pieces), top_value / len(pieces)))
        loudness = loudness * jnp.repeat(steps, dims[position] // blocks).reshape([-1 if axis == position else 1 for axis in range(len(dims))])
    return loudness


def profile(amount, total, most, slope):
    loads = [(1 << 20) // math.isqrt(rank ** slope) + 1 for rank in range(2, amount + 1)]
    spare, counts = total - most - (amount - 1), [1] * (amount - 1)
    while spare > 0:
        candidates = [i for i in range(amount - 1) if counts[i] < most]
        mass, budget = sum([loads[i] for i in candidates]), spare
        for i in candidates:
            extra = min(most - counts[i], max(1, budget * loads[i] // mass), spare)
            counts[i] = counts[i] + extra
            spare = spare - extra
    return np.array([most] + counts)


def uneven(own_key, number_of, total, most, slope):
    if number_of == 2:
        one = jax.random.randint(own_key, (), max(1, total - most), min(most, total - 1) + 1)
        return jnp.stack([one, total - one])
    sizes = jnp.asarray(profile(number_of, total, most, slope), jnp.int32)
    twos = (number_of - 1) // 2
    donor, receiver = sizes[1:1 + 2 * twos:2], sizes[2:2 + 2 * twos:2]
    slack = jnp.minimum(donor - 1, most - receiver)
    passed = jax.random.randint(jax.random.fold_in(own_key, 1), (twos,), 0, 1 << 20) % (slack + 1)
    sizes = sizes.at[1:1 + 2 * twos:2].set(donor - passed).at[2:2 + 2 * twos:2].set(receiver + passed)
    return sizes[jax.random.permutation(jax.random.fold_in(own_key, 2), number_of)]


def gaussian(rng, extent, width, bound, pieces=(), held_as=jnp.bfloat16):
    array = width * jax.random.normal(rng, extent, jnp.float32)
    if pieces:
        array = array * level_of(rng, extent, pieces, -0.22, 0.18)
    return jnp.clip(array, -bound, bound).astype(held_as)


def setup_inputs(seed: int = 0) -> dict:
    streams_of = jax.random.split(jax.random.key(seed), 5)
    return {
        "queries": draw_queries(jax.random.fold_in(streams_of[4], 71), 0),
        "keys": draw_keys(jax.random.fold_in(streams_of[4], 71), 0),
        "values": gaussian(streams_of[2], (TOKENS, KV_HEADS, HD), 1.0, 6.0, ((0, 16), (1, 2))),
        "seg_ids": jnp.searchsorted(jnp.cumsum(uneven(streams_of[3], NDOCS, TOKENS, DOC_MAX, 2)), jnp.arange(TOKENS), side="right").astype(jnp.int32),
    }


def reference(queries, keys, values, seg_ids):
    group_size = HEADS // KV_HEADS
    reach = STEPS * TOK_DEV
    window = (STEPS + 1) * TOK_DEV
    key_pad = jnp.concatenate([jnp.zeros((reach, KV_HEADS, HD), jnp.float32), keys.astype(jnp.float32)], axis=0)
    val_pad = jnp.concatenate([jnp.zeros((reach, KV_HEADS, HD), jnp.float32), values.astype(jnp.float32)], axis=0)
    seg_pad = jnp.concatenate([jnp.full((reach,), -1, jnp.int32), seg_ids.astype(jnp.int32)], axis=0)
    tile_count = TOKENS // TOK_DEV

    def one_tile(index):
        first = (index * TOK_DEV).astype(jnp.int32)
        query_tile = lax.dynamic_slice_in_dim(queries, first, TOK_DEV, 0).astype(jnp.float32)
        query_seg = lax.dynamic_slice_in_dim(seg_ids, first, TOK_DEV, 0)
        key_win = lax.dynamic_slice_in_dim(key_pad, first, window, 0)
        val_win = lax.dynamic_slice_in_dim(val_pad, first, window, 0)
        seg_win = lax.dynamic_slice_in_dim(seg_pad, first, window, 0)
        query_pos = first + jnp.arange(TOK_DEV, dtype=jnp.int32)
        key_pos = first - reach + jnp.arange(window, dtype=jnp.int32)
        mask = (query_seg[:, None] == seg_win[None, :]) & (key_pos[None, :] <= query_pos[:, None])
        grouped = query_tile.reshape(TOK_DEV, KV_HEADS, group_size, HD)
        scores = jnp.einsum("qkgd,skd->kgqs", grouped, key_win) * (HD ** -0.5)
        scores = jnp.where(mask, scores, -1e30)
        top = jnp.max(scores, axis=-1, keepdims=True)
        weights = jnp.where(mask, jnp.exp(scores - top), 0.0)
        total = jnp.sum(weights, axis=-1)
        rounded = lax.optimization_barrier(weights.astype(jnp.bfloat16)).astype(jnp.float32)
        summed = jnp.einsum("kgqs,skd->kgqd", rounded, val_win)
        result = summed / total[..., None]
        return result.transpose(2, 0, 1, 3).reshape(TOK_DEV, HEADS, HD).astype(jnp.bfloat16)

    tiles = lax.map(one_tile, jnp.arange(tile_count, dtype=jnp.int32))
    return tiles.reshape(TOKENS, HEADS, HD)
```

```python
import functools

import jax
import jax.numpy as jnp
from jax import lax
from jax.experimental import pallas as pl
from jax.experimental.pallas import tpu as pltpu
from jax.sharding import PartitionSpec as P

STEPS = 3
CHUNKS = 2
TOK_BLOCK = 64
SUB_ROWS = 256
MASKED = -1e30
LOG2E = 1.4426950408889634


def kernel(
    count, ctx, tok, kv, group, head_dim,
    q_hbm, k_hbm, v_hbm, seg_hbm, o_hbm,
    q_in, held, seg, plain, key_t, val_t, q_t, bias, top, total, acc, out,
    send_sem, recv_sem, seg_send, seg_recv, local_sem, out_sem,
):
    me = lax.axis_index("dcn") * ctx + lax.axis_index("ctx")

    def device(position):
        return {"dcn": position // ctx, "ctx": position % ctx}

    right = lax.rem(me + 1, count)
    left = lax.rem(me + count - 1, count)
    has_right = me < count - 1

    half = tok // CHUNKS

    def pass_chunk(d, which, c):
        rows = pl.ds(c * half * kv, half * kv)
        source = (k_hbm, v_hbm)[which].at[rows] if d == 0 else held.at[d, which, rows]
        return pltpu.make_async_remote_copy(
            src_ref=source,
            dst_ref=held.at[d + 1, which, rows],
            send_sem=send_sem.at[d, which, c],
            recv_sem=recv_sem.at[d, which, c],
            device_id=device(right),
            device_id_type=pl.DeviceIdType.MESH,
        )

    def pass_seg(d):
        return pltpu.make_async_remote_copy(
            src_ref=seg_hbm if d == 0 else seg.at[d],
            dst_ref=seg.at[d + 1],
            send_sem=seg_send.at[d],
            recv_sem=seg_recv.at[d],
            device_id=device(right),
            device_id_type=pl.DeviceIdType.MESH,
        )

    loads = [
        pltpu.make_async_copy(seg_hbm, seg.at[0], local_sem.at[0]),
        pltpu.make_async_copy(k_hbm, held.at[0, 0], local_sem.at[1]),
        pltpu.make_async_copy(v_hbm, held.at[0, 1], local_sem.at[2]),
        pltpu.make_async_copy(q_hbm, q_in, local_sem.at[3]),
    ]
    for load in loads:
        load.start()

    barrier = pltpu.get_barrier_semaphore()
    for neighbour in (left, right):
        pl.semaphore_signal(
            barrier, inc=1, device_id=device(neighbour), device_id_type=pl.DeviceIdType.MESH
        )
    pl.semaphore_wait(barrier, 2)

    order = [(c, which) for c in reversed(range(CHUNKS)) for which in range(2)]

    @pl.when(has_right)
    def _():
        pass_seg(0).start()
        for c, which in order:
            pass_chunk(0, which, c).start()

    for load in loads:
        load.wait()

    def split_queries(block, carry):
        tokens = pl.ds(pl.multiple_of(block * TOK_BLOCK, TOK_BLOCK), TOK_BLOCK)
        rows = pl.ds(pl.multiple_of(block * TOK_BLOCK * group, TOK_BLOCK * group), TOK_BLOCK * group)
        for pair in range(kv // 2):
            both = q_in[tokens, pl.ds(pair * 2 * group, 2 * group), :].astype(jnp.float32)
            for i in range(2):
                one = both[:, i * group:(i + 1) * group, :]
                q_t[2 * pair + i, rows, :] = one.reshape(TOK_BLOCK * group, head_dim).astype(jnp.bfloat16)
        return carry

    lax.fori_loop(0, tok // TOK_BLOCK, split_queries, 0)

    own_row = seg[0].astype(jnp.float32)
    at_row = lax.broadcasted_iota(jnp.int32, (tok, tok), 0)
    at_col = lax.broadcasted_iota(jnp.int32, (tok, tok), 1)
    own_col = jnp.sum(jnp.where(at_row == at_col, own_row, 0.0), axis=1, keepdims=True)

    def set_bias(d):
        ok = own_col == seg[d].astype(jnp.float32)
        if d == 0:
            ok = ok & (at_col <= at_row)
        one = jnp.where(ok, 0.0, MASKED)
        bias[...] = jnp.broadcast_to(one[:, None, :], (tok, group, tok)).reshape(tok * group, tok)

    def split_heads(d, key0, keys):
        rows = pl.ds(key0 * kv, keys * kv)
        for which, dest in ((0, key_t), (1, val_t)):
            plain[which, rows, :] = held[d, which, rows, :].astype(jnp.float32)
            for g in range(kv):
                dest[g, pl.ds(key0, keys), :] = plain[
                    which, pl.ds(key0 * kv + g, keys, stride=kv), :
                ].astype(jnp.bfloat16)

    factor = head_dim ** (-0.5) * LOG2E

    def attend(key0, keys, tokens, first):
        blocks = tokens // TOK_BLOCK
        span = TOK_BLOCK * group
        parts = keys // 128

        def body(step, carry):
            g = step // blocks
            base = (step % blocks) * span
            k = key_t[g, pl.ds(key0, keys), :]
            v = val_t[g, pl.ds(key0, keys), :]
            for sub in range(span // SUB_ROWS):
                rows = pl.ds(pl.multiple_of(base + sub * SUB_ROWS, SUB_ROWS), SUB_ROWS)
                s = lax.dot_general(
                    q_t[g, rows, :], k, (((1,), (1,)), ((), ())),
                    preferred_element_type=jnp.float32,
                )
                s = s * factor + bias[rows, pl.ds(key0, keys)]
                high = jnp.broadcast_to(jnp.max(s, axis=1, keepdims=True), (SUB_ROWS, 128))
                if not first:
                    before = top[g, rows, :]
                    high = jnp.maximum(high, before)
                weights = [jnp.exp2(s[:, i * 128:(i + 1) * 128] - high) for i in range(parts)]
                summed = functools.reduce(jnp.add, weights)
                w = jnp.concatenate([x.astype(jnp.bfloat16) for x in weights], axis=1)
                update = jnp.dot(w, v, preferred_element_type=jnp.float32)
                if not first:
                    rescale = jnp.exp2(before - high)
                    summed = summed + total[g, rows, :] * rescale
                    update = update + acc[g, rows, :] * rescale
                top[g, rows, :] = high
                total[g, rows, :] = summed
                acc[g, rows, :] = update
            return carry

        lax.fori_loop(0, kv * blocks, body, 0)

    set_bias(0)
    split_heads(0, 0, tok)
    attend(0, tok, tok, True)

    for d in range(1, STEPS + 1):
        @pl.when(me >= d)
        def _(d=d):
            pass_seg(d - 1).wait_recv()
            if d < STEPS:
                @pl.when(has_right)
                def _():
                    pass_seg(d).start()
            set_bias(d)
            for c in reversed(range(CHUNKS)):
                for which in range(2):
                    pass_chunk(d - 1, which, c).wait_recv()
                    if d < STEPS:
                        @pl.when(has_right)
                        def _(which=which, c=c):
                            pass_chunk(d, which, c).start()
                if d == STEPS:
                    split_heads(d, c * half, half)
                    attend(c * half, half, (c + 1) * half, False)
            if d < STEPS:
                split_heads(d, 0, tok)
                attend(0, tok, tok, False)

    def finish(block, carry):
        tokens = pl.ds(pl.multiple_of(block * TOK_BLOCK, TOK_BLOCK), TOK_BLOCK)
        rows = pl.ds(pl.multiple_of(block * TOK_BLOCK * group, TOK_BLOCK * group), TOK_BLOCK * group)
        for pair in range(kv // 2):
            done = []
            for i in range(2):
                g = 2 * pair + i
                whole = jnp.sum(total[g, rows, :], axis=1, keepdims=True)
                done.append((acc[g, rows, :] / whole).reshape(TOK_BLOCK, group, head_dim))
            out[tokens, pl.ds(pair * 2 * group, 2 * group), :] = jnp.concatenate(done, axis=1).astype(jnp.bfloat16)
        return carry

    lax.fori_loop(0, tok // TOK_BLOCK, finish, 0)
    write = pltpu.make_async_copy(out, o_hbm, out_sem)
    write.start()

    for d in range(STEPS):
        @pl.when(has_right & (me >= d))
        def _(d=d):
            pass_seg(d).wait_send()
            for c, which in order:
                pass_chunk(d, which, c).wait_send()
    write.wait()


def local(queries, keys, values, seg_ids):
    tok, heads, head_dim = queries.shape
    kv = keys.shape[1]
    group = heads // kv
    ctx = lax.axis_size("ctx")
    count = lax.axis_size("dcn") * ctx
    rows = tok * group
    bf16, f32 = jnp.bfloat16, jnp.float32
    return pl.pallas_call(
        functools.partial(kernel, count, ctx, tok, kv, group, head_dim),
        out_shape=jax.ShapeDtypeStruct((tok, heads, head_dim), bf16),
        in_specs=[pl.BlockSpec(memory_space=pltpu.HBM)] * 4,
        out_specs=pl.BlockSpec(memory_space=pltpu.HBM),
        scratch_shapes=[
            pltpu.VMEM((tok, heads, head_dim), bf16),
            pltpu.VMEM((STEPS + 1, 2, tok * kv, head_dim), bf16),
            pltpu.VMEM((STEPS + 1, 1, tok), jnp.int32),
            pltpu.VMEM((2, tok * kv, head_dim), f32),
            pltpu.VMEM((kv, tok, head_dim), bf16),
            pltpu.VMEM((kv, tok, head_dim), bf16),
            pltpu.VMEM((kv, rows, head_dim), bf16),
            pltpu.VMEM((rows, tok), f32),
            pltpu.VMEM((kv, rows, 128), f32),
            pltpu.VMEM((kv, rows, 128), f32),
            pltpu.VMEM((kv, rows, head_dim), f32),
            pltpu.VMEM((tok, heads, head_dim), bf16),
            pltpu.SemaphoreType.DMA((STEPS, 2, CHUNKS)),
            pltpu.SemaphoreType.DMA((STEPS, 2, CHUNKS)),
            pltpu.SemaphoreType.DMA((STEPS,)),
            pltpu.SemaphoreType.DMA((STEPS,)),
            pltpu.SemaphoreType.DMA((4,)),
            pltpu.SemaphoreType.DMA,
        ],
        compiler_params=pltpu.CompilerParams(
            collective_id=0, has_side_effects=True, vmem_limit_bytes=56 * 1024 * 1024
        ),
    )(
        queries,
        keys.reshape(tok * kv, head_dim),
        values.reshape(tok * kv, head_dim),
        seg_ids.reshape(1, tok),
    )


def solution(mesh):
    placed = (
        P(("dcn", "ctx"), "head", None),
        P(("dcn", "ctx"), "head", None),
        P(("dcn", "ctx"), "head", None),
        P(("dcn", "ctx")),
    )
    return jax.shard_map(
        local,
        mesh=mesh,
        in_specs=placed,
        out_specs=P(("dcn", "ctx"), "head", None),
        check_vma=False,
    )
```

```python
import functools

import jax
import jax.numpy as jnp
from jax import lax
from jax.experimental import pallas as pl
from jax.experimental.pallas import tpu as pltpu
from jax.sharding import PartitionSpec as P

STEPS = 3
CHUNKS = 2
TOK_BLOCK = 128
PART = 32
SUB_ROWS = 256
MASKED = -1e30
LOG2E = 1.4426950408889634


def kernel(
    count, ctx, tok, kv, group, head_dim,
    q_hbm, k_hbm, v_hbm, seg_hbm, o_hbm,
    q_in, held, seg, plain, key_t, val_t, q_t, bias, top, total, acc, out,
    send_sem, recv_sem, seg_send, seg_recv, local_sem, out_sem,
):
    me = lax.axis_index("dcn") * ctx + lax.axis_index("ctx")

    def device(position):
        return {"dcn": position // ctx, "ctx": position % ctx}

    right = lax.rem(me + 1, count)
    left = lax.rem(me + count - 1, count)
    has_right = me < count - 1

    half = tok // CHUNKS

    def pass_chunk(d, which, c):
        rows = pl.ds(c * half * kv, half * kv)
        source = (k_hbm, v_hbm)[which].at[rows] if d == 0 else held.at[d, which, rows]
        return pltpu.make_async_remote_copy(
            src_ref=source,
            dst_ref=held.at[d + 1, which, rows],
            send_sem=send_sem.at[d, which, c],
            recv_sem=recv_sem.at[d, which, c],
            device_id=device(right),
            device_id_type=pl.DeviceIdType.MESH,
        )

    def pass_seg(d):
        return pltpu.make_async_remote_copy(
            src_ref=seg_hbm if d == 0 else seg.at[d],
            dst_ref=seg.at[d + 1],
            send_sem=seg_send.at[d],
            recv_sem=seg_recv.at[d],
            device_id=device(right),
            device_id_type=pl.DeviceIdType.MESH,
        )

    loads = [
        pltpu.make_async_copy(seg_hbm, seg.at[0], local_sem.at[0]),
        pltpu.make_async_copy(k_hbm, held.at[0, 0], local_sem.at[1]),
        pltpu.make_async_copy(v_hbm, held.at[0, 1], local_sem.at[2]),
        pltpu.make_async_copy(q_hbm, q_in, local_sem.at[3]),
    ]
    for load in loads:
        load.start()

    barrier = pltpu.get_barrier_semaphore()
    for neighbour in (left, right):
        pl.semaphore_signal(
            barrier, inc=1, device_id=device(neighbour), device_id_type=pl.DeviceIdType.MESH
        )
    pl.semaphore_wait(barrier, 2)

    order = [(c, which) for c in reversed(range(CHUNKS)) for which in range(2)]

    @pl.when(has_right)
    def _():
        pass_seg(0).start()
        for c, which in order:
            pass_chunk(0, which, c).start()

    for load in loads:
        load.wait()

    def split_queries(block, carry):
        tokens = pl.ds(pl.multiple_of(block * TOK_BLOCK, TOK_BLOCK), TOK_BLOCK)
        rows = pl.ds(pl.multiple_of(block * TOK_BLOCK * group, TOK_BLOCK * group), TOK_BLOCK * group)
        for pair in range(kv // 2):
            both = q_in[tokens, pl.ds(pair * 2 * group, 2 * group), :].astype(jnp.float32)
            for i in range(2):
                one = both[:, i * group:(i + 1) * group, :]
                q_t[2 * pair + i, rows, :] = one.reshape(TOK_BLOCK * group, head_dim).astype(jnp.bfloat16)
        return carry

    lax.fori_loop(0, tok // TOK_BLOCK, split_queries, 0)

    own_row = seg[0].astype(jnp.float32)
    at_row = lax.broadcasted_iota(jnp.int32, (tok, tok), 0)
    at_col = lax.broadcasted_iota(jnp.int32, (tok, tok), 1)
    own_col = jnp.sum(jnp.where(at_row == at_col, own_row, 0.0), axis=1, keepdims=True)

    def set_bias(d):
        ok = own_col == seg[d].astype(jnp.float32)
        if d == 0:
            ok = ok & (at_col <= at_row)
        one = jnp.where(ok, 0.0, MASKED)
        bias[...] = jnp.broadcast_to(one[:, None, :], (tok, group, tok)).reshape(tok * group, tok)

    def split_heads(d, key0, keys):
        rows = pl.ds(key0 * kv, keys * kv)
        for which, dest in ((0, key_t), (1, val_t)):
            plain[which, rows, :] = held[d, which, rows, :].astype(jnp.float32)
            for g in range(kv):
                dest[g, pl.ds(key0, keys), :] = plain[
                    which, pl.ds(key0 * kv + g, keys, stride=kv), :
                ].astype(jnp.bfloat16)

    factor = head_dim ** (-0.5) * LOG2E

    def attend(key0, keys, tokens, first):
        blocks = tokens // TOK_BLOCK
        span = TOK_BLOCK * group
        parts = keys // 128

        def body(step, carry):
            g = step // blocks
            base = (step % blocks) * span
            k = key_t[g, pl.ds(key0, keys), :]
            v = val_t[g, pl.ds(key0, keys), :]
            spans = [
                pl.ds(pl.multiple_of(base + sub * SUB_ROWS, SUB_ROWS), SUB_ROWS)
                for sub in range(span // SUB_ROWS)
            ]
            results = []
            for rows in spans:
                s = lax.dot_general(
                    q_t[g, rows, :], k, (((1,), (1,)), ((), ())),
                    preferred_element_type=jnp.float32,
                )
                s = s * factor + bias[rows, pl.ds(key0, keys)]
                high = jnp.broadcast_to(jnp.max(s, axis=1, keepdims=True), (SUB_ROWS, 128))
                if not first:
                    before = top[g, rows, :]
                    high = jnp.maximum(high, before)
                weights = [jnp.exp2(s[:, i * 128:(i + 1) * 128] - high) for i in range(parts)]
                summed = functools.reduce(jnp.add, weights)
                w = jnp.concatenate([x.astype(jnp.bfloat16) for x in weights], axis=1)
                update = jnp.dot(w, v, preferred_element_type=jnp.float32)
                if not first:
                    rescale = jnp.exp2(before - high)
                    summed = summed + total[g, rows, :] * rescale
                    update = update + acc[g, rows, :] * rescale
                results.append((high, summed, update))
            for rows, (high, summed, update) in zip(spans, results):
                top[g, rows, :] = high
                total[g, rows, :] = summed
                acc[g, rows, :] = update
            return carry

        lax.fori_loop(0, kv * blocks, body, 0)

    set_bias(0)
    split_heads(0, 0, tok)
    attend(0, tok, tok, True)

    def receive(d, c):
        for which in range(2):
            pass_chunk(d - 1, which, c).wait_recv()
            if d < STEPS:
                @pl.when(has_right)
                def _(which=which):
                    pass_chunk(d, which, c).start()

    for d in range(1, STEPS + 1):
        @pl.when(me >= d)
        def _(d=d):
            pass_seg(d - 1).wait_recv()
            if d < STEPS:
                @pl.when(has_right)
                def _():
                    pass_seg(d).start()
            set_bias(d)
            if d < STEPS:
                for c in reversed(range(CHUNKS)):
                    receive(d, c)
                split_heads(d, 0, tok)
                attend(0, tok, tok, False)

    def finish(first_block, blocks):
        def body(block, carry):
            tokens = pl.ds(pl.multiple_of(block * PART, PART), PART)
            rows = pl.ds(pl.multiple_of(block * PART * group, PART * group), PART * group)
            for pair in range(kv // 2):
                done = []
                for i in range(2):
                    g = 2 * pair + i
                    whole = jnp.sum(total[g, rows, :], axis=1, keepdims=True)
                    done.append((acc[g, rows, :] / whole).reshape(PART, group, head_dim))
                out[tokens, pl.ds(pair * 2 * group, 2 * group), :] = (
                    jnp.concatenate(done, axis=1).astype(jnp.bfloat16)
                )
            return carry

        lax.fori_loop(first_block, first_block + blocks, body, 0)

    def write(c):
        tokens = pl.ds(c * half, half)
        return pltpu.make_async_copy(out.at[tokens], o_hbm.at[tokens], out_sem.at[c])

    for c in reversed(range(CHUNKS)):
        @pl.when(me >= STEPS)
        def _(c=c):
            receive(STEPS, c)
            split_heads(STEPS, c * half, half)
            attend(c * half, half, (c + 1) * half, False)

        finish(c * half // PART, half // PART)
        write(c).start()

    for d in range(STEPS):
        @pl.when(has_right & (me >= d))
        def _(d=d):
            pass_seg(d).wait_send()
            for c, which in order:
                pass_chunk(d, which, c).wait_send()
    for c in range(CHUNKS):
        write(c).wait()


def local(queries, keys, values, seg_ids):
    tok, heads, head_dim = queries.shape
    kv = keys.shape[1]
    group = heads // kv
    ctx = lax.axis_size("ctx")
    count = lax.axis_size("dcn") * ctx
    rows = tok * group
    bf16, f32 = jnp.bfloat16, jnp.float32
    return pl.pallas_call(
        functools.partial(kernel, count, ctx, tok, kv, group, head_dim),
        out_shape=jax.ShapeDtypeStruct((tok, heads, head_dim), bf16),
        in_specs=[pl.BlockSpec(memory_space=pltpu.HBM)] * 4,
        out_specs=pl.BlockSpec(memory_space=pltpu.HBM),
        scratch_shapes=[
            pltpu.VMEM((tok, heads, head_dim), bf16),
            pltpu.VMEM((STEPS + 1, 2, tok * kv, head_dim), bf16),
            pltpu.VMEM((STEPS + 1, 1, tok), jnp.int32),
            pltpu.VMEM((2, tok * kv, head_dim), f32),
            pltpu.VMEM((kv, tok, head_dim), bf16),
            pltpu.VMEM((kv, tok, head_dim), bf16),
            pltpu.VMEM((kv, rows, head_dim), bf16),
            pltpu.VMEM((rows, tok), f32),
            pltpu.VMEM((kv, rows, 128), f32),
            pltpu.VMEM((kv, rows, 128), f32),
            pltpu.VMEM((kv, rows, head_dim), f32),
            pltpu.VMEM((tok, heads, head_dim), bf16),
            pltpu.SemaphoreType.DMA((STEPS, 2, CHUNKS)),
            pltpu.SemaphoreType.DMA((STEPS, 2, CHUNKS)),
            pltpu.SemaphoreType.DMA((STEPS,)),
            pltpu.SemaphoreType.DMA((STEPS,)),
            pltpu.SemaphoreType.DMA((4,)),
            pltpu.SemaphoreType.DMA((CHUNKS,)),
        ],
        compiler_params=pltpu.CompilerParams(
            collective_id=0, has_side_effects=True, vmem_limit_bytes=56 * 1024 * 1024
        ),
    )(
        queries,
        keys.reshape(tok * kv, head_dim),
        values.reshape(tok * kv, head_dim),
        seg_ids.reshape(1, tok),
    )


def solution(mesh):
    placed = (
        P(("dcn", "ctx"), "head", None),
        P(("dcn", "ctx"), "head", None),
        P(("dcn", "ctx"), "head", None),
        P(("dcn", "ctx")),
    )
    return jax.shard_map(
        local,
        mesh=mesh,
        in_specs=placed,
        out_specs=P(("dcn", "ctx"), "head", None),
        check_vma=False,
    )
```

```python
import functools

import jax
import jax.numpy as jnp
from jax import lax
from jax.experimental import pallas as pl
from jax.experimental.pallas import tpu as pltpu
from jax.sharding import PartitionSpec as P

STEPS = 3
CHUNKS = 2
TOK_BLOCK = 256
PART = 32
SUB_ROWS = 256
MASKED = -1e30
LOG2E = 1.4426950408889634


def kernel(
    count, ctx, tok, kv, group, head_dim,
    q_hbm, k_hbm, v_hbm, seg_hbm, o_hbm,
    q_in, held, seg, plain, key_t, val_t, q_t, bias, top, total, acc, out,
    send_sem, recv_sem, seg_send, seg_recv, local_sem, out_sem,
):
    me = lax.axis_index("dcn") * ctx + lax.axis_index("ctx")

    def device(position):
        return {"dcn": position // ctx, "ctx": position % ctx}

    right = lax.rem(me + 1, count)
    left = lax.rem(me + count - 1, count)
    has_right = me < count - 1

    half = tok // CHUNKS

    def pass_chunk(d, which, c):
        rows = pl.ds(c * half * kv, half * kv)
        source = (k_hbm, v_hbm)[which].at[rows] if d == 0 else held.at[d, which, rows]
        return pltpu.make_async_remote_copy(
            src_ref=source,
            dst_ref=held.at[d + 1, which, rows],
            send_sem=send_sem.at[d, which, c],
            recv_sem=recv_sem.at[d, which, c],
            device_id=device(right),
            device_id_type=pl.DeviceIdType.MESH,
        )

    def pass_seg(d):
        return pltpu.make_async_remote_copy(
            src_ref=seg_hbm if d == 0 else seg.at[d],
            dst_ref=seg.at[d + 1],
            send_sem=seg_send.at[d],
            recv_sem=seg_recv.at[d],
            device_id=device(right),
            device_id_type=pl.DeviceIdType.MESH,
        )

    loads = [
        pltpu.make_async_copy(seg_hbm, seg.at[0], local_sem.at[0]),
        pltpu.make_async_copy(k_hbm, held.at[0, 0], local_sem.at[1]),
        pltpu.make_async_copy(v_hbm, held.at[0, 1], local_sem.at[2]),
        pltpu.make_async_copy(q_hbm, q_in, local_sem.at[3]),
    ]
    for load in loads:
        load.start()

    barrier = pltpu.get_barrier_semaphore()
    for neighbour in (left, right):
        pl.semaphore_signal(
            barrier, inc=1, device_id=device(neighbour), device_id_type=pl.DeviceIdType.MESH
        )
    pl.semaphore_wait(barrier, 2)

    order = [(c, which) for c in reversed(range(CHUNKS)) for which in range(2)]

    @pl.when(has_right)
    def _():
        pass_seg(0).start()
        for c, which in order:
            pass_chunk(0, which, c).start()

    for load in loads:
        load.wait()

    def split_queries(block, carry):
        tokens = pl.ds(pl.multiple_of(block * PART, PART), PART)
        rows = pl.ds(pl.multiple_of(block * PART * group, PART * group), PART * group)
        for pair in range(kv // 2):
            both = q_in[tokens, pl.ds(pair * 2 * group, 2 * group), :].astype(jnp.float32)
            for i in range(2):
                one = both[:, i * group:(i + 1) * group, :]
                q_t[2 * pair + i, rows, :] = one.reshape(PART * group, head_dim).astype(jnp.bfloat16)
        return carry

    lax.fori_loop(0, tok // PART, split_queries, 0)

    own_row = seg[0].astype(jnp.float32)
    at_row = lax.broadcasted_iota(jnp.int32, (tok, tok), 0)
    at_col = lax.broadcasted_iota(jnp.int32, (tok, tok), 1)
    own_col = jnp.sum(jnp.where(at_row == at_col, own_row, 0.0), axis=1, keepdims=True)

    def set_bias(d):
        ok = own_col == seg[d].astype(jnp.float32)
        if d == 0:
            ok = ok & (at_col <= at_row)
        one = jnp.where(ok, 0.0, MASKED)
        bias[...] = jnp.broadcast_to(one[:, None, :], (tok, group, tok)).reshape(tok * group, tok)

    def split_heads(d, key0, keys):
        rows = pl.ds(key0 * kv, keys * kv)
        for which, dest in ((0, key_t), (1, val_t)):
            plain[which, rows, :] = held[d, which, rows, :].astype(jnp.float32)
            for g in range(kv):
                dest[g, pl.ds(key0, keys), :] = plain[
                    which, pl.ds(key0 * kv + g, keys, stride=kv), :
                ].astype(jnp.bfloat16)

    factor = head_dim ** (-0.5) * LOG2E

    def attend(key0, keys, tokens, first):
        at_once = min(tokens, TOK_BLOCK)
        blocks = tokens // at_once
        span = at_once * group
        parts = keys // 128

        def body(step, carry):
            g = step // blocks
            base = (step % blocks) * span
            k = key_t[g, pl.ds(key0, keys), :]
            v = val_t[g, pl.ds(key0, keys), :]
            spans = [
                pl.ds(pl.multiple_of(base + sub * SUB_ROWS, SUB_ROWS), SUB_ROWS)
                for sub in range(span // SUB_ROWS)
            ]
            results = []
            for rows in spans:
                s = lax.dot_general(
                    q_t[g, rows, :], k, (((1,), (1,)), ((), ())),
                    preferred_element_type=jnp.float32,
                )
                s = s * factor + bias[rows, pl.ds(key0, keys)]
                high = jnp.broadcast_to(jnp.max(s, axis=1, keepdims=True), (SUB_ROWS, 128))
                if not first:
                    before = top[g, rows, :]
                    high = jnp.maximum(high, before)
                weights = [jnp.exp2(s[:, i * 128:(i + 1) * 128] - high) for i in range(parts)]
                summed = functools.reduce(jnp.add, weights)
                w = jnp.concatenate([x.astype(jnp.bfloat16) for x in weights], axis=1)
                update = jnp.dot(w, v, preferred_element_type=jnp.float32)
                if not first:
                    rescale = jnp.exp2(before - high)
                    summed = summed + total[g, rows, :] * rescale
                    update = update + acc[g, rows, :] * rescale
                results.append((high, summed, update))
            for rows, (high, summed, update) in zip(spans, results):
                top[g, rows, :] = high
                total[g, rows, :] = summed
                acc[g, rows, :] = update
            return carry

        lax.fori_loop(0, kv * blocks, body, 0)

    set_bias(0)
    split_heads(0, 0, tok)
    attend(0, tok, tok, True)

    def receive(d, c):
        for which in range(2):
            pass_chunk(d - 1, which, c).wait_recv()
            if d < STEPS:
                @pl.when(has_right)
                def _(which=which):
                    pass_chunk(d, which, c).start()

    for d in range(1, STEPS + 1):
        @pl.when(me >= d)
        def _(d=d):
            pass_seg(d - 1).wait_recv()
            if d < STEPS:
                @pl.when(has_right)
                def _():
                    pass_seg(d).start()
            set_bias(d)
            if d < STEPS:
                for c in reversed(range(CHUNKS)):
                    receive(d, c)
                split_heads(d, 0, tok)
                attend(0, tok, tok, False)

    def finish(first_block, blocks):
        def body(block, carry):
            tokens = pl.ds(pl.multiple_of(block * PART, PART), PART)
            rows = pl.ds(pl.multiple_of(block * PART * group, PART * group), PART * group)
            for pair in range(kv // 2):
                done = []
                for i in range(2):
                    g = 2 * pair + i
                    whole = jnp.sum(total[g, rows, :], axis=1, keepdims=True)
                    done.append((acc[g, rows, :] / whole).reshape(PART, group, head_dim))
                out[tokens, pl.ds(pair * 2 * group, 2 * group), :] = (
                    jnp.concatenate(done, axis=1).astype(jnp.bfloat16)
                )
            return carry

        lax.fori_loop(first_block, first_block + blocks, body, 0)

    def write(c):
        tokens = pl.ds(c * half, half)
        return pltpu.make_async_copy(out.at[tokens], o_hbm.at[tokens], out_sem.at[c])

    for c in reversed(range(CHUNKS)):
        @pl.when(me >= STEPS)
        def _(c=c):
            receive(STEPS, c)
            split_heads(STEPS, c * half, half)
            attend(c * half, half, (c + 1) * half, False)

        finish(c * half // PART, half // PART)
        write(c).start()

    for d in range(STEPS):
        @pl.when(has_right & (me >= d))
        def _(d=d):
            pass_seg(d).wait_send()
            for c, which in order:
                pass_chunk(d, which, c).wait_send()
    for c in range(CHUNKS):
        write(c).wait()


def local(queries, keys, values, seg_ids):
    tok, heads, head_dim = queries.shape
    kv = keys.shape[1]
    group = heads // kv
    ctx = lax.axis_size("ctx")
    count = lax.axis_size("dcn") * ctx
    rows = tok * group
    bf16, f32 = jnp.bfloat16, jnp.float32
    return pl.pallas_call(
        functools.partial(kernel, count, ctx, tok, kv, group, head_dim),
        out_shape=jax.ShapeDtypeStruct((tok, heads, head_dim), bf16),
        in_specs=[pl.BlockSpec(memory_space=pltpu.HBM)] * 4,
        out_specs=pl.BlockSpec(memory_space=pltpu.HBM),
        scratch_shapes=[
            pltpu.VMEM((tok, heads, head_dim), bf16),
            pltpu.VMEM((STEPS + 1, 2, tok * kv, head_dim), bf16),
            pltpu.VMEM((STEPS + 1, 1, tok), jnp.int32),
            pltpu.VMEM((2, tok * kv, head_dim), f32),
            pltpu.VMEM((kv, tok, head_dim), bf16),
            pltpu.VMEM((kv, tok, head_dim), bf16),
            pltpu.VMEM((kv, rows, head_dim), bf16),
            pltpu.VMEM((rows, tok), f32),
            pltpu.VMEM((kv, rows, 128), f32),
            pltpu.VMEM((kv, rows, 128), f32),
            pltpu.VMEM((kv, rows, head_dim), f32),
            pltpu.VMEM((tok, heads, head_dim), bf16),
            pltpu.SemaphoreType.DMA((STEPS, 2, CHUNKS)),
            pltpu.SemaphoreType.DMA((STEPS, 2, CHUNKS)),
            pltpu.SemaphoreType.DMA((STEPS,)),
            pltpu.SemaphoreType.DMA((STEPS,)),
            pltpu.SemaphoreType.DMA((4,)),
            pltpu.SemaphoreType.DMA((CHUNKS,)),
        ],
        compiler_params=pltpu.CompilerParams(
            collective_id=0, has_side_effects=True, vmem_limit_bytes=56 * 1024 * 1024
        ),
    )(
        queries,
        keys.reshape(tok * kv, head_dim),
        values.reshape(tok * kv, head_dim),
        seg_ids.reshape(1, tok),
    )


def solution(mesh):
    placed = (
        P(("dcn", "ctx"), "head", None),
        P(("dcn", "ctx"), "head", None),
        P(("dcn", "ctx"), "head", None),
        P(("dcn", "ctx")),
    )
    return jax.shard_map(
        local,
        mesh=mesh,
        in_specs=placed,
        out_specs=P(("dcn", "ctx"), "head", None),
        check_vma=False,
    )
```
